32 devices in a mesh: group: 2 (over x), gx: 16 (over z, y, core).
Axes of the slice: x: 2, y: 2, z: 4, core: 2. Of those that a mesh axis runs over, the one named last changes fastest.
Arguments:
- tokens: bfloat16 [8192, 768], P('gx', 'group'), parts along dimension 1, may hold values from -190 to 190, as said below
- norm_gain: bfloat16 [8192], P('gx'), may hold values from 0.099609375 to 1.8984375
- gate_weight: bfloat16 [16, 2048, 8192], P('gx'), may hold values from -0.0625 to 0.0625
- up_weight: bfloat16 [16, 2048, 8192], P('gx'), may hold values from -0.0625 to 0.0625
- down_weight: bfloat16 [16, 8192, 2048], P('gx'), may hold values from -0.03125 to 0.03125
Outputs:
- output: bfloat16 [8192, 768], P('gx', 'group'), parts along dimension 1
The draws below stay inside these ranges and needn't reach their ends.
There are 2 independent parts, one for each index of `group`. The reference program is written for one: setup_inputs(seed, part) draws one part's arguments, and reference() takes and returns one part's arrays. A program takes and returns all parts, laid end to end along the dimension named above; an argument that names none is the same for every part. Nothing has to cross between parts.
Inputs may be any that keep to these rules, and one draw needn't show every extreme that they name: `tokens`: activations of a batch.
All inputs are finite; a program needn't handle non-finite values.
Results may differ from the reference program's by a relative error of at most 0.0065.
Values may be sent and summed in bfloat16 or wider, within the bound.
A program may use at most 320 MiB of HBM per device.

```python
import jax
import jax.numpy as jnp
from jax import lax

D = 8192
FF = 32768
ROWS = 384
GA = 4
GB = 4
N_GX = 16


def draw_tokens(key, part):
    key = jax.random.fold_in(key, 11)
    key_values, key_columns, key_rows = jax.random.split(key, 3)
    position = jnp.arange(D, dtype=jnp.float32)[:, None] / D
    jitter = jax.random.uniform(key_columns, (D, 1), jnp.float32)
    entries = jax.random.truncated_normal(key_values, -6.0, 6.0, (D, ROWS), jnp.float32)
    column_scale = 10.0 ** (0.5 * position + 0.5 * jitter)
    row_scale = 10.0 ** jax.random.uniform(key_rows, (1, ROWS), jnp.float32, -0.5, 0.5)
    return (entries * column_scale * row_scale).astype(jnp.bfloat16)


def level_of(rng, dims, cuts, low, largest):
    def one(axis_at, shards_of):
        draws = jax.random.uniform(jax.random.fold_in(jax.random.fold_in(rng, 6), axis_at), (shards_of,), jnp.float32, low / len(cuts), largest / len(cuts))
        return jnp.repeat(jnp.exp(draws), dims[axis_at] // shards_of).reshape((-1,) + (1,) * (len(dims) - axis_at - 1))

    level = one(*cuts[0])
    for cut in cuts[1:]:
        level = level * one(*cut)
    return level


def scatter_about(own_key, dims, scale, bound, pieces=(), held_as=jnp.bfloat16):
    drawn = jax.random.normal(own_key, dims, jnp.float32) * scale
    if len(pieces) > 0:
        drawn = level_of(own_key, dims, pieces, -0.22, 0.18) * drawn
    return jnp.clip(drawn, min=-bound, max=bound).astype(held_as)


def setup_inputs(seed: int = 0, part: int = 0) -> dict:
    key_list = jax.random.split(jax.random.key(seed), 6)
    own_keys = jax.random.split(jax.random.fold_in(key_list[5], part), 6)
    tokens = draw_tokens(jax.random.fold_in(jax.random.fold_in(key_list[5], part), 71), part)
    norm_gain = jnp.clip(1.0 + 0.18 * jax.random.normal(key_list[1], (D,), jnp.float32), 0.099609375, 1.8984375).astype(jnp.bfloat16)
    gate_weight = scatter_about(key_list[2], (N_GX, D // GA, FF // GB), D ** -0.5, 0.0625, ((0, 16),))
    up_weight = scatter_about(key_list[3], (N_GX, D // GA, FF // GB), D ** -0.5, 0.0625, ((0, 16),))
    down_weight = scatter_about(key_list[4], (N_GX, FF // GB, D // GA), FF ** -0.5, 0.03125, ((0, 16),))
    return {"tokens": tokens, "norm_gain": norm_gain, "gate_weight": gate_weight, "up_weight": up_weight, "down_weight": down_weight}


def reference(tokens, norm_gain, gate_weight, up_weight, down_weight):
    values = tokens.astype(jnp.float32)
    inverse = lax.rsqrt(lax.optimization_barrier(jnp.mean(values * values, axis=0, keepdims=True)) + 1e-05)
    normed = (values * inverse * norm_gain.astype(jnp.float32)[:, None]).astype(jnp.bfloat16)
    normed_blocks = normed.reshape(GA, D // GA, ROWS)
    inward = (((0, 2), (0, 1)), ((), ()))
    gate_tiles = gate_weight.reshape(GA, GB, D // GA, FF // GB)
    up_tiles = up_weight.reshape(GA, GB, D // GA, FF // GB)
    gate_sum = lax.dot_general(gate_tiles, normed_blocks, inward, preferred_element_type=jnp.float32).reshape(FF, ROWS)
    up_sum = lax.dot_general(up_tiles, normed_blocks, inward, preferred_element_type=jnp.float32).reshape(FF, ROWS)
    hidden = (jax.nn.silu(gate_sum) * up_sum).astype(jnp.bfloat16)
    hidden_blocks = hidden.reshape(GB, FF // GB, ROWS)
    down_tiles = down_weight.reshape(GA, GB, FF // GB, D // GA)
    outward = (((1, 2), (0, 1)), ((), ()))
    output = lax.dot_general(down_tiles, hidden_blocks, outward, preferred_element_type=jnp.float32).reshape(D, ROWS)
    return output.astype(jnp.bfloat16)
```

```python
import functools

import jax
import jax.numpy as jnp
from jax import lax
from jax.experimental import pallas as pl
from jax.experimental.pallas import tpu as pltpu
from jax.sharding import PartitionSpec as P

GA = 4
CHUNK = 128
SKEW = 2
F32 = jnp.float32
BF16 = jnp.bfloat16


def kernel(
    count,
    tok_ref,
    gain_ref,
    gate_ref,
    up_ref,
    down_ref,
    out_ref,
    ssq,
    gath,
    norm_t,
    part,
    red,
    hid,
    wgu,
    wdn,
    acc,
    final,
    send_buf,
    recv_buf,
    sq_send,
    sq_recv,
    ga_send,
    ga_recv,
    red_send,
    red_recv,
    hid_send,
    hid_recv,
    wg_sem,
    wu_sem,
    wd_sem,
    fin_send,
    fin_recv,
):
    blocks = count // GA
    shard, rows = tok_ref.shape
    width = shard * blocks
    units = gate_ref.shape[2]
    half = units // 2
    steps = half // CHUNK
    last = GA - 1
    me = lax.axis_index("gx")
    a = me // blocks
    b = me % blocks

    def remote(src, dst, send, recv, to):
        return pltpu.make_async_remote_copy(
            src_ref=src,
            dst_ref=dst,
            send_sem=send,
            recv_sem=recv,
            device_id={"gx": to},
            device_id_type=pl.DeviceIdType.MESH,
        )

    roles = (a, last - a)
    nexts = (me + blocks, me - blocks)
    prevs = (me - blocks, me + blocks)

    def wide_copies(d, k, slot):
        cols = pl.ds(pl.multiple_of(d * half + k * CHUNK, CHUNK), CHUNK)
        return (
            pltpu.make_async_copy(
                gate_ref.at[0, :, cols], wgu.at[d, slot, :, pl.ds(0, CHUNK)], wg_sem.at[d, slot]
            ),
            pltpu.make_async_copy(
                up_ref.at[0, :, cols], wgu.at[d, slot, :, pl.ds(CHUNK, CHUNK)], wu_sem.at[d, slot]
            ),
        )

    def down_copy(d, k, slot):
        lines = pl.ds(pl.multiple_of(d * half + k * CHUNK, CHUNK), CHUNK)
        return pltpu.make_async_copy(down_ref.at[0, lines, :], wdn.at[d, slot], wd_sem.at[d, slot])

    def red_copy(d, k):
        slot = red.at[d, k]
        return remote(slot, slot, red_send.at[d, k], red_recv.at[d, k], nexts[d])

    def hid_copy(d, k):
        slot = hid.at[d, k]
        return remote(slot, slot, hid_send.at[d, k], hid_recv.at[d, k], prevs[d])

    barrier = pltpu.get_barrier_semaphore()

    @pl.loop(1, count)
    def _(j):
        pl.semaphore_signal(
            barrier,
            inc=1,
            device_id={"gx": (me + j) % count},
            device_id_type=pl.DeviceIdType.MESH,
        )

    for d in range(2):
        for copy in wide_copies(d, 0, 0):
            copy.start()
        down_copy(d, 0, 0).start()

    values = tok_ref[...].astype(F32)
    ssq[me] = jnp.sum((values * values).reshape(shard // 8, 8, rows), axis=0)
    pl.semaphore_wait(barrier, count - 1)

    def sq_copy(owner, to):
        return remote(ssq.at[owner], ssq.at[owner], sq_send.at[to], sq_recv.at[owner], to)

    @pl.loop(1, count)
    def _(j):
        sq_copy(me, (me + j) % count).start()

    @pl.loop(1, count)
    def _(j):
        other = (me + j) % count
        sq_copy(other, other).wait_recv()

    squares = jnp.sum(jnp.sum(ssq[...], axis=0), axis=0, keepdims=True)
    inverse = lax.rsqrt(squares / (shard * count) + 1e-05)
    normed = (values * inverse * gain_ref[...].astype(F32)).astype(BF16)

    def lines_of(index):
        return pl.ds(pl.multiple_of(index * shard, shard), shard)

    gath[lines_of(b), :] = normed

    def gath_copy(owner, to):
        lines = gath.at[lines_of(owner), :]
        return remote(lines, lines, ga_send.at[to], ga_recv.at[owner], a * blocks + to)

    @pl.loop(1, blocks)
    def _(j):
        gath_copy(b, (b + j) % blocks).start()

    acc[...] = jnp.zeros_like(acc)

    @pl.loop(1, count)
    def _(j):
        sq_copy(me, (me + j) % count).wait_send()

    @pl.loop(1, blocks)
    def _(j):
        other = (b + j) % blocks
        gath_copy(other, other).wait_recv()

    @pl.loop(1, blocks)
    def _(j):
        gath_copy(b, (b + j) % blocks).wait_send()

    for at in range(0, width, 256):
        norm_t[:, at : at + 256] = gath[at : at + 256, :].T

    @pl.loop(0, steps + 2 * last * SKEW)
    def _(i):
        for d in range(2):
            r = roles[d]
            k = i - SKEW * (last + last - r)

            @pl.when((k >= 0) & (k < steps) & (r < last))
            def _(d=d, r=r, k=k):
                hid_copy(d, k).wait_recv()

                @pl.when(r > 0)
                def _():
                    hid_copy(d, k).start()

        for d in range(2):
            r = roles[d]
            k = i - SKEW * r

            @pl.when((k >= 0) & (k < steps))
            def _(d=d, r=r, k=k):
                slot = lax.rem(k, 2)
                for copy in wide_copies(d, k, slot):
                    copy.wait()

                @pl.when(k + 1 < steps)
                def _():
                    for copy in wide_copies(d, k + 1, 1 - slot):
                        copy.start()

                part[...] = jnp.dot(norm_t[...], wgu[d, slot], preferred_element_type=F32)

                @pl.when(r > 0)
                def _():
                    red_copy(d, k).wait_recv()

                @pl.when(r == 0)
                def _():
                    red[d, k] = part[...].astype(BF16)

                @pl.when((r > 0) & (r < last))
                def _():
                    red[d, k] = (part[...] + red[d, k].astype(F32)).astype(BF16)

                @pl.when(r < last)
                def _():
                    red_copy(d, k).start()

                @pl.when(r == last)
                def _():
                    total = part[...] + red[d, k].astype(F32)
                    gate = total[:, :CHUNK]
                    hid[d, k] = (gate / (1.0 + jnp.exp(-gate)) * total[:, CHUNK:]).astype(BF16)
                    hid_copy(d, k).start()

        for d in range(2):
            r = roles[d]
            k = i - SKEW * (last + last - r)

            @pl.when((k >= 0) & (k < steps))
            def _(d=d, r=r, k=k):
                slot = lax.rem(k, 2)
                down_copy(d, k, slot).wait()

                @pl.when(k + 1 < steps)
                def _():
                    down_copy(d, k + 1, 1 - slot).start()

                acc[...] += jnp.dot(hid[d, k], wdn[d, slot], preferred_element_type=F32)

    bits = blocks.bit_length() - 1

    def flipped(t):
        return (b >> t) & 1

    def slice_of(t, u, digit):
        return (u << (t + 1)) + digit * (1 << t) + b % (1 << t)

    def turned(index):
        if shard % 128 == 0:
            return acc[:, lines_of(index)].T
        return final[lines_of(index), :]

    if shard % 128 != 0:
        final[...] = acc[...].T

    base = 0
    for t in range(bits):
        many = blocks >> (t + 1)
        mine = flipped(t)
        partner = me + (1 - 2 * mine) * (1 << t)
        copies = []
        for u in range(many):
            index = slice_of(t, u, 1 - mine)
            source = turned(index) if t == 0 else final[lines_of(index), :]
            send_buf[base + u] = source.astype(BF16)
            copy = remote(
                send_buf.at[base + u],
                recv_buf.at[base + u],
                fin_send.at[base + u],
                fin_recv.at[base + u],
                partner,
            )
            copy.start()
            copies.append(copy)
        if t == 0 and shard % 128 == 0:
            for u in range(many):
                index = slice_of(t, u, mine)
                final[lines_of(index), :] = turned(index)
        for u, copy in enumerate(copies):
            copy.wait()
            lines = lines_of(slice_of(t, u, mine))
            final[lines, :] = final[lines, :] + recv_buf[base + u].astype(F32)
        base += many
    out_ref[...] = final[lines_of(b), :].astype(BF16)

    for d in range(2):
        r = roles[d]

        @pl.loop(0, steps)
        def _(k, d=d, r=r):
            @pl.when(r < last)
            def _():
                red_copy(d, k).wait_send()

            @pl.when(r > 0)
            def _():
                hid_copy(d, k).wait_send()


def shards(tokens, norm_gain, gate_weight, up_weight, down_weight):
    count = lax.axis_size("gx")
    blocks = count // GA
    shard, rows = tokens.shape
    width = shard * blocks
    steps = gate_weight.shape[2] // 2 // CHUNK
    dma = pltpu.SemaphoreType.DMA
    vmem = pl.BlockSpec(memory_space=pltpu.VMEM)
    hbm = pl.BlockSpec(memory_space=pl.ANY)
    return pl.pallas_call(
        functools.partial(kernel, count),
        out_shape=jax.ShapeDtypeStruct((shard, rows), BF16),
        in_specs=[vmem, vmem, hbm, hbm, hbm],
        out_specs=vmem,
        scratch_shapes=[
            pltpu.VMEM((count, 8, rows), F32),
            pltpu.VMEM((width, rows), BF16),
            pltpu.VMEM((rows, width), BF16),
            pltpu.VMEM((rows, 2 * CHUNK), F32),
            pltpu.VMEM((2, steps, rows, 2 * CHUNK), BF16),
            pltpu.VMEM((2, steps, rows, CHUNK), BF16),
            pltpu.VMEM((2, 2, width, 2 * CHUNK), BF16),
            pltpu.VMEM((2, 2, CHUNK, width), BF16),
            pltpu.VMEM((rows, width), F32),
            pltpu.VMEM((width, rows), F32),
            pltpu.VMEM((blocks - 1, shard, rows), BF16),
            pltpu.VMEM((blocks - 1, shard, rows), BF16),
            dma((count,)),
            dma((count,)),
            dma((blocks,)),
            dma((blocks,)),
            dma((2, steps)),
            dma((2, steps)),
            dma((2, steps)),
            dma((2, steps)),
            dma((2, 2)),
            dma((2, 2)),
            dma((2, 2)),
            dma((blocks - 1,)),
            dma((blocks - 1,)),
        ],
        compiler_params=pltpu.CompilerParams(
            collective_id=0, has_side_effects=True, vmem_limit_bytes=56 * 1024 * 1024
        ),
        cost_estimate=pl.CostEstimate(
            flops=6 * width * rows * gate_weight.shape[2],
            bytes_accessed=6 * width * gate_weight.shape[2],
            transcendentals=0,
        ),
    )(tokens, norm_gain[:, None], gate_weight, up_weight, down_weight)


def solution(mesh):
    placed = (
        P("gx", "group"),
        P("gx"),
        P("gx", None, None),
        P("gx", None, None),
        P("gx", None, None),
    )
    return jax.shard_map(
        shards, mesh=mesh, in_specs=placed, out_specs=P("gx", "group"), check_vma=False
    )
```

```python
import functools

import jax
import jax.numpy as jnp
from jax import lax
from jax.experimental import pallas as pl
from jax.experimental.pallas import tpu as pltpu
from jax.sharding import PartitionSpec as P

GA = 4
CHUNK = 128
SKEW = 2
BACK = 2
F32 = jnp.float32
BF16 = jnp.bfloat16


def kernel(
    count,
    tok_ref,
    gain_ref,
    gate_ref,
    up_ref,
    down_ref,
    out_ref,
    ssq,
    gains,
    gath,
    norm_t,
    part,
    red,
    hid,
    wgu,
    wdn,
    acc,
    final,
    send_buf,
    recv_buf,
    sq_send,
    sq_recv,
    gain_send,
    gain_recv,
    ga_send,
    ga_recv,
    red_send,
    red_recv,
    hid_send,
    hid_recv,
    wg_sem,
    wu_sem,
    wd_sem,
    fin_send,
    fin_recv,
):
    blocks = count // GA
    shard, rows = tok_ref.shape
    width = shard * blocks
    units = gate_ref.shape[2]
    half = units // 2
    steps = half // CHUNK
    last = GA - 1
    me = lax.axis_index("gx")
    a = me // blocks
    b = me % blocks

    def remote(src, dst, send, recv, to):
        return pltpu.make_async_remote_copy(
            src_ref=src,
            dst_ref=dst,
            send_sem=send,
            recv_sem=recv,
            device_id={"gx": to},
            device_id_type=pl.DeviceIdType.MESH,
        )

    roles = (a, last - a)
    nexts = (me + blocks, me - blocks)
    prevs = (me - blocks, me + blocks)

    def wide_copies(d, k, slot):
        cols = pl.ds(pl.multiple_of(d * half + k * CHUNK, CHUNK), CHUNK)
        return (
            pltpu.make_async_copy(
                gate_ref.at[0, :, cols], wgu.at[d, slot, :, pl.ds(0, CHUNK)], wg_sem.at[d, slot]
            ),
            pltpu.make_async_copy(
                up_ref.at[0, :, cols], wgu.at[d, slot, :, pl.ds(CHUNK, CHUNK)], wu_sem.at[d, slot]
            ),
        )

    def down_copy(d, k, slot):
        lines = pl.ds(pl.multiple_of(d * half + k * CHUNK, CHUNK), CHUNK)
        return pltpu.make_async_copy(down_ref.at[0, lines, :], wdn.at[d, slot], wd_sem.at[d, slot])

    def red_copy(d, k):
        slot = red.at[d, k]
        return remote(slot, slot, red_send.at[d, k], red_recv.at[d, k], nexts[d])

    def hid_copy(d, k):
        slot = hid.at[d, k]
        return remote(slot, slot, hid_send.at[d, k], hid_recv.at[d, k], prevs[d])

    barrier = pltpu.get_barrier_semaphore()

    @pl.loop(1, count)
    def _(j):
        pl.semaphore_signal(
            barrier,
            inc=1,
            device_id={"gx": (me + j) % count},
            device_id_type=pl.DeviceIdType.MESH,
        )

    for d in range(2):
        for copy in wide_copies(d, 0, 0):
            copy.start()
        down_copy(d, 0, 0).start()

    def lines_of(index):
        return pl.ds(pl.multiple_of(index * shard, shard), shard)

    bits = blocks.bit_length() - 1
    plan = []
    for t in reversed(range(bits)):
        plan.append((t, (blocks >> (t + 1)) - 1, blocks >> (t + 1)))

    def sq_copy(owner, to):
        return remote(ssq.at[owner], ssq.at[owner], sq_send.at[to], sq_recv.at[owner], to)

    def gain_copy(owner, to):
        row = gains.at[owner]
        return remote(row, row, gain_send.at[to], gain_recv.at[owner], a * blocks + to)

    def gath_copy(t, base, u, theirs):
        digit = (b >> t) & 1
        held = 1 - digit if theirs else digit
        index = u * (1 << (t + 1)) + held * (1 << t) + b % (1 << t)
        lines = gath.at[lines_of(index), :]
        partner = me + (1 - 2 * digit) * (1 << t)
        return index, remote(lines, lines, ga_send.at[base + u], ga_recv.at[base + u], partner)

    def turn(index):
        if shard % 128 == 0:
            norm_t[:, lines_of(index)] = gath[lines_of(index), :].T

    gath[lines_of(b), :] = tok_ref[...]
    gains[b] = jnp.broadcast_to(gain_ref[...], gains.shape[1:])
    values = tok_ref[...].astype(F32)
    ssq[me] = jnp.sum((values * values).reshape(shard // 8, 8, rows), axis=0)
    pl.semaphore_wait(barrier, count - 1)

    @pl.loop(1, count)
    def _(j):
        sq_copy(me, (me + j) % count).start()

    @pl.loop(1, blocks)
    def _(j):
        gain_copy(b, (b + j) % blocks).start()

    for t, base, many in plan:
        gath_copy(t, base, b >> (t + 1), False)[1].start()

    acc[...] = jnp.zeros_like(acc)
    pending = [b]
    for t, base, many in plan:
        own = b >> (t + 1)
        for j in range(1, many):
            gath_copy(t, base, (own + j) % many, False)[1].start()
        for index in pending:
            turn(index)
        pending = []
        for u in range(many):
            index, copy = gath_copy(t, base, u, True)
            copy.wait_recv()
            pending.append(index)
    for index in pending:
        turn(index)
    if shard % 128 != 0:
        norm_t[...] = gath[...].T

    @pl.loop(1, count)
    def _(j):
        other = (me + j) % count
        sq_copy(other, other).wait_recv()

    @pl.loop(1, blocks)
    def _(j):
        other = (b + j) % blocks
        gain_copy(other, other).wait_recv()

    squares = jnp.sum(jnp.sum(ssq[...], axis=0), axis=0, keepdims=True)
    inverse = lax.rsqrt(squares / (shard * count) + 1e-05)
    column = jnp.broadcast_to(inverse, (128, rows)).T[:, :1]
    for q in range(blocks):
        lanes = slice(q * shard, (q + 1) * shard)
        norm_t[:, lanes] = (norm_t[:, lanes].astype(F32) * column * gains[q, :1, :]).astype(BF16)

    @pl.loop(0, steps + last * (SKEW + BACK))
    def _(i):
        for d in range(2):
            r = roles[d]
            k = i - SKEW * last - BACK * (last - r)

            @pl.when((k >= 0) & (k < steps) & (r < last))
            def _(d=d, r=r, k=k):
                hid_copy(d, k).wait_recv()

                @pl.when(r > 0)
                def _():
                    hid_copy(d, k).start()

        for d in range(2):
            r = roles[d]
            k = i - SKEW * r

            @pl.when((k >= 0) & (k < steps))
            def _(d=d, r=r, k=k):
                slot = lax.rem(k, 2)
                for copy in wide_copies(d, k, slot):
                    copy.wait()

                @pl.when(k + 1 < steps)
                def _():
                    for copy in wide_copies(d, k + 1, 1 - slot):
                        copy.start()

                part[...] = jnp.dot(norm_t[...], wgu[d, slot], preferred_element_type=F32)

                @pl.when(r > 0)
                def _():
                    red_copy(d, k).wait_recv()

                @pl.when(r == 0)
                def _():
                    red[d, k] = part[...].astype(BF16)

                @pl.when((r > 0) & (r < last))
                def _():
                    red[d, k] = (part[...] + red[d, k].astype(F32)).astype(BF16)

                @pl.when(r < last)
                def _():
                    red_copy(d, k).start()

                @pl.when(r == last)
                def _():
                    total = part[...] + red[d, k].astype(F32)
                    gate = total[:, :CHUNK]
                    hid[d, k] = (gate / (1.0 + jnp.exp(-gate)) * total[:, CHUNK:]).astype(BF16)
                    hid_copy(d, k).start()

        for d in range(2):
            r = roles[d]
            k = i - SKEW * last - BACK * (last - r)

            @pl.when((k >= 0) & (k < steps))
            def _(d=d, r=r, k=k):
                slot = lax.rem(k, 2)
                down_copy(d, k, slot).wait()

                @pl.when(k + 1 < steps)
                def _():
                    down_copy(d, k + 1, 1 - slot).start()

                acc[...] += jnp.dot(hid[d, k], wdn[d, slot], preferred_element_type=F32)

    def flipped(t):
        return (b >> t) & 1

    def slice_of(t, u, digit):
        return (u << (t + 1)) + digit * (1 << t) + b % (1 << t)

    def turned(index):
        if shard % 128 == 0:
            return acc[:, lines_of(index)].T
        return final[lines_of(index), :]

    if shard % 128 != 0:
        final[...] = acc[...].T

    base = 0
    for t in range(bits):
        many = blocks >> (t + 1)
        mine = flipped(t)
        partner = me + (1 - 2 * mine) * (1 << t)
        copies = []
        for u in range(many):
            index = slice_of(t, u, 1 - mine)
            source = turned(index) if t == 0 else final[lines_of(index), :]
            send_buf[base + u] = source.astype(BF16)
            copy = remote(
                send_buf.at[base + u],
                recv_buf.at[base + u],
                fin_send.at[base + u],
                fin_recv.at[base + u],
                partner,
            )
            copy.start()
            copies.append(copy)
        if t == 0 and shard % 128 == 0:
            for u in range(many):
                index = slice_of(t, u, mine)
                final[lines_of(index), :] = turned(index)
        for u, copy in enumerate(copies):
            copy.wait()
            lines = lines_of(slice_of(t, u, mine))
            final[lines, :] = final[lines, :] + recv_buf[base + u].astype(F32)
        base += many
    out_ref[...] = final[lines_of(b), :].astype(BF16)

    @pl.loop(1, count)
    def _(j):
        sq_copy(me, (me + j) % count).wait_send()

    @pl.loop(1, blocks)
    def _(j):
        gain_copy(b, (b + j) % blocks).wait_send()

    for t, base, many in plan:
        for u in range(many):
            gath_copy(t, base, u, False)[1].wait_send()

    for d in range(2):
        r = roles[d]

        @pl.loop(0, steps)
        def _(k, d=d, r=r):
            @pl.when(r < last)
            def _():
                red_copy(d, k).wait_send()

            @pl.when(r > 0)
            def _():
                hid_copy(d, k).wait_send()


def shards(tokens, norm_gain, gate_weight, up_weight, down_weight):
    count = lax.axis_size("gx")
    blocks = count // GA
    shard, rows = tokens.shape
    width = shard * blocks
    steps = gate_weight.shape[2] // 2 // CHUNK
    dma = pltpu.SemaphoreType.DMA
    vmem = pl.BlockSpec(memory_space=pltpu.VMEM)
    hbm = pl.BlockSpec(memory_space=pl.ANY)
    return pl.pallas_call(
        functools.partial(kernel, count),
        out_shape=jax.ShapeDtypeStruct((shard, rows), BF16),
        in_specs=[vmem, vmem, hbm, hbm, hbm],
        out_specs=vmem,
        scratch_shapes=[
            pltpu.VMEM((count, 8, rows), F32),
            pltpu.VMEM((blocks, 8, shard), F32),
            pltpu.VMEM((width, rows), BF16),
            pltpu.VMEM((rows, width), BF16),
            pltpu.VMEM((rows, 2 * CHUNK), F32),
            pltpu.VMEM((2, steps, rows, 2 * CHUNK), BF16),
            pltpu.VMEM((2, steps, rows, CHUNK), BF16),
            pltpu.VMEM((2, 2, width, 2 * CHUNK), BF16),
            pltpu.VMEM((2, 2, CHUNK, width), BF16),
            pltpu.VMEM((rows, width), F32),
            pltpu.VMEM((width, rows), F32),
            pltpu.VMEM((blocks - 1, shard, rows), BF16),
            pltpu.VMEM((blocks - 1, shard, rows), BF16),
            dma((count,)),
            dma((count,)),
            dma((blocks,)),
            dma((blocks,)),
            dma((blocks,)),
            dma((blocks,)),
            dma((2, steps)),
            dma((2, steps)),
            dma((2, steps)),
            dma((2, steps)),
            dma((2, 2)),
            dma((2, 2)),
            dma((2, 2)),
            dma((blocks - 1,)),
            dma((blocks - 1,)),
        ],
        compiler_params=pltpu.CompilerParams(
            collective_id=0, has_side_effects=True, vmem_limit_bytes=56 * 1024 * 1024
        ),
        cost_estimate=pl.CostEstimate(
            flops=6 * width * rows * gate_weight.shape[2],
            bytes_accessed=6 * width * gate_weight.shape[2],
            transcendentals=0,
        ),
    )(tokens, norm_gain.astype(F32)[None, :], gate_weight, up_weight, down_weight)


def solution(mesh):
    placed = (
        P("gx", "group"),
        P("gx"),
        P("gx", None, None),
        P("gx", None, None),
        P("gx", None, None),
    )
    return jax.shard_map(
        shards, mesh=mesh, in_specs=placed, out_specs=P("gx", "group"), check_vma=False
    )
```

```python
import functools

import jax
import jax.numpy as jnp
from jax import lax
from jax.experimental import pallas as pl
from jax.experimental.pallas import tpu as pltpu
from jax.sharding import PartitionSpec as P

GA = 4
CHUNK = 128
SKEW = 2
BACK = 2
F32 = jnp.float32
BF16 = jnp.bfloat16


def kernel(
    count,
    tok_ref,
    gain_ref,
    gate_ref,
    up_ref,
    down_ref,
    out_ref,
    ssq,
    gains,
    gath,
    norm_t,
    part,
    red,
    hid,
    wgu,
    wdn,
    acc,
    final,
    send_buf,
    recv_buf,
    sq_send,
    sq_recv,
    gain_send,
    gain_recv,
    ga_send,
    ga_recv,
    red_send,
    red_recv,
    hid_send,
    hid_recv,
    wg_sem,
    wu_sem,
    wd_sem,
    fin_send,
    fin_recv,
):
    blocks = count // GA
    shard, rows = tok_ref.shape
    width = shard * blocks
    units = gate_ref.shape[2]
    half = units // 2
    steps = half // CHUNK
    last = GA - 1
    me = lax.axis_index("gx")
    a = me // blocks
    b = me % blocks

    def remote(src, dst, send, recv, to):
        return pltpu.make_async_remote_copy(
            src_ref=src,
            dst_ref=dst,
            send_sem=send,
            recv_sem=recv,
            device_id={"gx": to},
            device_id_type=pl.DeviceIdType.MESH,
        )

    roles = (a, last - a)
    nexts = (me + blocks, me - blocks)
    prevs = (me - blocks, me + blocks)

    def wide_copies(d, k, slot):
        cols = pl.ds(pl.multiple_of(d * half + k * CHUNK, CHUNK), CHUNK)
        return (
            pltpu.make_async_copy(
                gate_ref.at[0, :, cols], wgu.at[d, slot, :, pl.ds(0, CHUNK)], wg_sem.at[d, slot]
            ),
            pltpu.make_async_copy(
                up_ref.at[0, :, cols], wgu.at[d, slot, :, pl.ds(CHUNK, CHUNK)], wu_sem.at[d, slot]
            ),
        )

    def down_copy(d, k, slot):
        lines = pl.ds(pl.multiple_of(d * half + k * CHUNK, CHUNK), CHUNK)
        return pltpu.make_async_copy(down_ref.at[0, lines, :], wdn.at[d, slot], wd_sem.at[d, slot])

    def red_copy(d, k):
        slot = red.at[d, k]
        return remote(slot, slot, red_send.at[d, k], red_recv.at[d, k], nexts[d])

    def hid_copy(d, k):
        slot = hid.at[d, k]
        return remote(slot, slot, hid_send.at[d, k], hid_recv.at[d, k], prevs[d])

    barrier = pltpu.get_barrier_semaphore()

    @pl.loop(1, count)
    def _(j):
        pl.semaphore_signal(
            barrier,
            inc=1,
            device_id={"gx": (me + j) % count},
            device_id_type=pl.DeviceIdType.MESH,
        )

    for d in range(2):
        for copy in wide_copies(d, 0, 0):
            copy.start()
        down_copy(d, 0, 0).start()

    def lines_of(index):
        return pl.ds(pl.multiple_of(index * shard, shard), shard)

    bits = blocks.bit_length() - 1
    plan = []
    for t in reversed(range(bits)):
        plan.append((t, (blocks >> (t + 1)) - 1, blocks >> (t + 1)))

    def sq_copy(owner, to):
        return remote(ssq.at[owner], ssq.at[owner], sq_send.at[to], sq_recv.at[owner], to)

    def gain_copy(owner, to):
        row = gains.at[owner]
        return remote(row, row, gain_send.at[to], gain_recv.at[owner], a * blocks + to)

    def gath_copy(t, base, u, theirs):
        digit = (b >> t) & 1
        held = 1 - digit if theirs else digit
        index = u * (1 << (t + 1)) + held * (1 << t) + b % (1 << t)
        lines = gath.at[lines_of(index), :]
        partner = me + (1 - 2 * digit) * (1 << t)
        return index, remote(lines, lines, ga_send.at[base + u], ga_recv.at[base + u], partner)

    def turn(index):
        if shard % 128 == 0:
            norm_t[:, lines_of(index)] = gath[lines_of(index), :].T

    gath[lines_of(b), :] = tok_ref[...]
    gains[b] = jnp.broadcast_to(gain_ref[...], gains.shape[1:])
    values = tok_ref[...].astype(F32)
    ssq[me] = jnp.sum((values * values).reshape(shard // 8, 8, rows), axis=0)
    pl.semaphore_wait(barrier, count - 1)

    @pl.loop(1, count)
    def _(j):
        sq_copy(me, (me + j) % count).start()

    @pl.loop(1, blocks)
    def _(j):
        gain_copy(b, (b + j) % blocks).start()

    for t, base, many in plan:
        gath_copy(t, base, b >> (t + 1), False)[1].start()

    acc[...] = jnp.zeros_like(acc)
    pending = [b]
    for t, base, many in plan:
        own = b >> (t + 1)
        for j in range(1, many):
            gath_copy(t, base, (own + j) % many, False)[1].start()
        for index in pending:
            turn(index)
        pending = []
        for u in range(many):
            index, copy = gath_copy(t, base, u, True)
            copy.wait_recv()
            pending.append(index)
    for index in pending:
        turn(index)
    if shard % 128 != 0:
        norm_t[...] = gath[...].T

    @pl.loop(1, count)
    def _(j):
        other = (me + j) % count
        sq_copy(other, other).wait_recv()

    @pl.loop(1, blocks)
    def _(j):
        other = (b + j) % blocks
        gain_copy(other, other).wait_recv()

    squares = jnp.sum(jnp.sum(ssq[...], axis=0), axis=0, keepdims=True)
    inverse = lax.rsqrt(squares / (shard * count) + 1e-05)
    column = jnp.broadcast_to(inverse, (128, rows)).T[:, :1]
    for q in range(blocks):
        lanes = slice(q * shard, (q + 1) * shard)
        norm_t[:, lanes] = (norm_t[:, lanes].astype(F32) * column * gains[q, :1, :]).astype(BF16)

    @pl.loop(0, steps + last * (SKEW + BACK))
    def _(i):
        for d in range(2):
            r = roles[d]
            k = i - SKEW * r

            @pl.when((k >= 0) & (k < steps))
            def _(d=d, r=r, k=k):
                slot = lax.rem(k, 2)
                for copy in wide_copies(d, k, slot):
                    copy.wait()

                @pl.when(k + 1 < steps)
                def _():
                    for copy in wide_copies(d, k + 1, 1 - slot):
                        copy.start()

                part[...] = jnp.dot(norm_t[...], wgu[d, slot], preferred_element_type=F32)

                @pl.when(r > 0)
                def _():
                    red_copy(d, k).wait_recv()

                @pl.when(r == 0)
                def _():
                    red[d, k] = part[...].astype(BF16)

                @pl.when((r > 0) & (r < last))
                def _():
                    red[d, k] = (part[...] + red[d, k].astype(F32)).astype(BF16)

                @pl.when(r < last)
                def _():
                    red_copy(d, k).start()

                @pl.when(r == last)
                def _():
                    total = part[...] + red[d, k].astype(F32)
                    gate = total[:, :CHUNK]
                    hid[d, k] = (gate / (1.0 + jnp.exp(-gate)) * total[:, CHUNK:]).astype(BF16)
                    hid_copy(d, k).start()

        for d in range(2):
            r = roles[d]
            k = i - SKEW * last - BACK * (last - r)

            @pl.when((k >= 0) & (k < steps) & (r < last))
            def _(d=d, r=r, k=k):
                hid_copy(d, k).wait_recv()

                @pl.when(r > 0)
                def _():
                    hid_copy(d, k).start()

        for d in range(2):
            r = roles[d]
            k = i - SKEW * last - BACK * (last - r)

            @pl.when((k >= 0) & (k < steps))
            def _(d=d, r=r, k=k):
                slot = lax.rem(k, 2)
                down_copy(d, k, slot).wait()

                @pl.when(k + 1 < steps)
                def _():
                    down_copy(d, k + 1, 1 - slot).start()

                acc[...] += jnp.dot(hid[d, k], wdn[d, slot], preferred_element_type=F32)

    def flipped(t):
        return (b >> t) & 1

    def slice_of(t, u, digit):
        return (u << (t + 1)) + digit * (1 << t) + b % (1 << t)

    def turned(index):
        if shard % 128 == 0:
            return acc[:, lines_of(index)].T
        return final[lines_of(index), :]

    if shard % 128 != 0:
        final[...] = acc[...].T

    base = 0
    for t in range(bits):
        many = blocks >> (t + 1)
        mine = flipped(t)
        partner = me + (1 - 2 * mine) * (1 << t)
        copies = []
        for u in range(many):
            index = slice_of(t, u, 1 - mine)
            source = turned(index) if t == 0 else final[lines_of(index), :]
            send_buf[base + u] = source.astype(BF16)
            copy = remote(
                send_buf.at[base + u],
                recv_buf.at[base + u],
                fin_send.at[base + u],
                fin_recv.at[base + u],
                partner,
            )
            copy.start()
            copies.append(copy)
        if t == 0 and shard % 128 == 0:
            for u in range(many):
                index = slice_of(t, u, mine)
                final[lines_of(index), :] = turned(index)
        for u, copy in enumerate(copies):
            copy.wait()
            lines = lines_of(slice_of(t, u, mine))
            final[lines, :] = final[lines, :] + recv_buf[base + u].astype(F32)
        base += many
    out_ref[...] = final[lines_of(b), :].astype(BF16)

    @pl.loop(1, count)
    def _(j):
        sq_copy(me, (me + j) % count).wait_send()

    @pl.loop(1, blocks)
    def _(j):
        gain_copy(b, (b + j) % blocks).wait_send()

    for t, base, many in plan:
        for u in range(many):
            gath_copy(t, base, u, False)[1].wait_send()

    for d in range(2):
        r = roles[d]

        @pl.loop(0, steps)
        def _(k, d=d, r=r):
            @pl.when(r < last)
            def _():
                red_copy(d, k).wait_send()

            @pl.when(r > 0)
            def _():
                hid_copy(d, k).wait_send()


def shards(tokens, norm_gain, gate_weight, up_weight, down_weight):
    count = lax.axis_size("gx")
    blocks = count // GA
    shard, rows = tokens.shape
    width = shard * blocks
    steps = gate_weight.shape[2] // 2 // CHUNK
    dma = pltpu.SemaphoreType.DMA
    vmem = pl.BlockSpec(memory_space=pltpu.VMEM)
    hbm = pl.BlockSpec(memory_space=pl.ANY)
    return pl.pallas_call(
        functools.partial(kernel, count),
        out_shape=jax.ShapeDtypeStruct((shard, rows), BF16),
        in_specs=[vmem, vmem, hbm, hbm, hbm],
        out_specs=vmem,
        scratch_shapes=[
            pltpu.VMEM((count, 8, rows), F32),
            pltpu.VMEM((blocks, 8, shard), F32),
            pltpu.VMEM((width, rows), BF16),
            pltpu.VMEM((rows, width), BF16),
            pltpu.VMEM((rows, 2 * CHUNK), F32),
            pltpu.VMEM((2, steps, rows, 2 * CHUNK), BF16),
            pltpu.VMEM((2, steps, rows, CHUNK), BF16),
            pltpu.VMEM((2, 2, width, 2 * CHUNK), BF16),
            pltpu.VMEM((2, 2, CHUNK, width), BF16),
            pltpu.VMEM((rows, width), F32),
            pltpu.VMEM((width, rows), F32),
            pltpu.VMEM((blocks - 1, shard, rows), BF16),
            pltpu.VMEM((blocks - 1, shard, rows), BF16),
            dma((count,)),
            dma((count,)),
            dma((blocks,)),
            dma((blocks,)),
            dma((blocks,)),
            dma((blocks,)),
            dma((2, steps)),
            dma((2, steps)),
            dma((2, steps)),
            dma((2, steps)),
            dma((2, 2)),
            dma((2, 2)),
            dma((2, 2)),
            dma((blocks - 1,)),
            dma((blocks - 1,)),
        ],
        compiler_params=pltpu.CompilerParams(
            collective_id=0, has_side_effects=True, vmem_limit_bytes=56 * 1024 * 1024
        ),
        cost_estimate=pl.CostEstimate(
            flops=6 * width * rows * gate_weight.shape[2],
            bytes_accessed=6 * width * gate_weight.shape[2],
            transcendentals=0,
        ),
    )(tokens, norm_gain.astype(F32)[None, :], gate_weight, up_weight, down_weight)


def solution(mesh):
    placed = (
        P("gx", "group"),
        P("gx"),
        P("gx", None, None),
        P("gx", None, None),
        P("gx", None, None),
    )
    return jax.shard_map(
        shards, mesh=mesh, in_specs=placed, out_specs=P("gx", "group"), check_vma=False
    )
```
